256 devices in a mesh: row: 32 (over x_hi, z, core), cent: 8 (over y, x_lo).
Axes of the slice: x: 4 (x_hi: 2, x_lo: 2; x = x_hi * 2 + x_lo), y: 4, z: 8, core: 2. Of those that a mesh axis runs over, the one named last changes fastest.
Arguments:
- embedding_pool: bfloat16 [262144, 512], P('row')
- select_index: int32 [131072], P('row'), may hold values from 0 to 8191
- seed_index: int32 [4096], P('cent'), may hold values from 0 to 131071
Outputs:
- centroids: bfloat16 [4096, 512], P('cent')
- row_energy: float32 [131072], P('row')
The draws below stay inside these ranges and needn't reach their ends.
All inputs are finite; a program needn't handle non-finite values.
Results may differ from the reference program's by a relative error of at most 0.0036.
Values may be sent and summed in bfloat16 or wider, within the bound.
A program may use at most 64 MiB of HBM per device.

```python
import jax
import jax.numpy as jnp
from jax import lax

D = 512
K = 4096
ITERS = 2
ROW_DEV = 4096
POOL_DEV = 8192
ROWS = 131072
POOL = 262144
N_ROW = 32


def draw_embedding_pool(key, part):
    key = jax.random.fold_in(key, 11)
    key_vals, key_scale = jax.random.split(key, 2)
    values = jax.random.normal(key_vals, (POOL, D), jnp.float32)
    scale = jnp.exp(jax.random.uniform(key_scale, (POOL, 1), jnp.float32, 0.0, jnp.log(4.0)))
    values = values * scale
    return values.astype(jnp.bfloat16)


def plant(drawn, key, smallest, high):
    dims = drawn.shape
    spot = [jax.random.randint(jax.random.fold_in(key, axis), (), 0, dims[axis]) for axis in range(len(dims))]
    drawn = drawn.at[tuple(spot)].set(smallest)
    longest = dims.index(max(dims))
    spot[longest] = (spot[longest] + 1) % dims[longest]
    return drawn.at[tuple(spot)].set(high)


def setup_inputs(seed: int = 0) -> dict:
    keys = jax.random.split(jax.random.key(seed), 4)
    return {
        "embedding_pool": draw_embedding_pool(jax.random.fold_in(keys[3], 71), 0),
        "select_index": plant(jax.random.randint(keys[1], (ROWS,), 0, POOL_DEV), jax.random.fold_in(keys[1], 1), 0, POOL_DEV - 1).astype(jnp.int32),
        "seed_index": plant(jax.random.randint(keys[2], (K,), 0, ROWS), jax.random.fold_in(keys[2], 1), 0, ROWS - 1).astype(jnp.int32),
    }


def normalize(vectors):
    return vectors * lax.rsqrt(lax.optimization_barrier(jnp.sum(vectors * vectors, axis=1, keepdims=True)) + 1e-06)

def reference(embedding_pool, select_index, seed_index):
    block_of = jnp.arange(ROWS, dtype=jnp.int32) // ROW_DEV
    sample = embedding_pool[(block_of * POOL_DEV + select_index).astype(jnp.int32)]
    centers = normalize(sample[seed_index].astype(jnp.float32)).astype(jnp.bfloat16)
    blocked = sample.reshape(N_ROW, ROW_DEV, D)
    energy = jnp.zeros((N_ROW, ROW_DEV), jnp.float32)
    for iteration in range(ITERS):

        def one_block(sums, block_rows):
            scores = jnp.dot(block_rows, centers.T, preferred_element_type=jnp.float32)
            top = lax.optimization_barrier(jnp.max(scores, axis=1))
            expo = jnp.exp(scores - top[:, None])
            total = lax.optimization_barrier(jnp.sum(expo, axis=1))
            weights = expo / total[:, None]
            probs = weights.astype(jnp.bfloat16)
            sums = sums + jnp.dot(probs.T, block_rows, preferred_element_type=jnp.float32)
            return (sums, top + jnp.log(total))
        sums, energy = lax.scan(one_block, jnp.zeros((K, D), jnp.float32), blocked)
        centers = normalize(sums).astype(jnp.bfloat16)
    return (centers, energy.reshape(ROWS))
```

```python
import jax
import jax.numpy as jnp
from jax import lax
from jax.experimental import pallas as pl
from jax.experimental.pallas import tpu as pltpu
from jax.sharding import PartitionSpec as P

F32 = jnp.float32
BF16 = jnp.bfloat16
MESH = pl.DeviceIdType.MESH

POOL = 8192
ROWS = 4096
CENT = 512
D = 512
LANES = 128
PARTS = D // LANES
LOADS = 8
BLOCK = 512
BLOCKS = ROWS // BLOCK
GROUPS = 4
GROUP = ROWS // GROUPS
OWN = 16
Z = 8
CENTS = 8
FAR_FIRST = (4, 3, 5, 2, 6, 1, 7)


def rows(start, size):
    return pl.ds(pl.multiple_of(start, size), size)


def kernel(
    pool_hbm,
    select,
    seed,
    centers_out,
    energy_out,
    pool_in,
    pool32,
    sample32,
    sample,
    seeds32,
    expo,
    scores,
    stats,
    scale,
    sums,
    seeds16,
    core16,
    x16,
    xs16,
    z16,
    zs16,
    own32,
    core32,
    x32,
    xs32,
    z32,
    zs32,
    centers,
    load_sem,
    rs_send,
    rs_recv,
    ag_send,
    ag_recv,
    stat_send,
    stat_recv,
):
    row = lax.axis_index("row")
    cent = lax.axis_index("cent")
    xh = row // 16
    z = (row // 2) % Z
    core = row % 2

    def row_id(xh_, z_, core_):
        return xh_ * 16 + z_ * 2 + core_

    sibling = (row_id(xh, z, 1 - core), cent)
    across = (row_id(1 - xh, z, core), cent)

    def z_id(distance):
        return (row_id(xh, (z + distance) % Z, core), cent)

    def cent_id(distance):
        return (row, (cent + distance) % CENTS)

    sent = []

    def send(src, dst, send_sem, recv_sem, device):
        copy = pltpu.make_async_remote_copy(
            src_ref=src, dst_ref=dst, send_sem=send_sem, recv_sem=recv_sem,
            device_id=device, device_id_type=MESH,
        )
        copy.start()
        sent.append(copy)

    def arrived(dst, send_sem, recv_sem, device):
        pltpu.make_async_remote_copy(
            src_ref=dst, dst_ref=dst, send_sem=send_sem, recv_sem=recv_sem,
            device_id=device, device_id_type=MESH,
        ).wait_recv()

    step = POOL // LOADS
    loads = []
    for i in range(LOADS):
        part = pl.ds(i * step, step)
        copy = pltpu.make_async_copy(pool_hbm.at[part], pool_in.at[part], load_sem.at[i])
        copy.start()
        loads.append(copy)
    barrier = pltpu.get_barrier_semaphore()
    partners = [sibling, across] + [z_id(d) for d in range(1, Z)] + [cent_id(d) for d in range(1, CENTS)]
    for partner in partners:
        pl.semaphore_signal(barrier, inc=1, device_id=partner, device_id_type=MESH)

    for i in range(LOADS):
        loads[i].wait()

        def widen(b, carry, i=i):
            start = i * step + b * 32
            block = pool_in[rows(start, 32), :].astype(F32)
            for t in range(PARTS):
                pool32[pl.ds(start * PARTS + t, 32, stride=PARTS), :] = block[:, t * LANES : (t + 1) * LANES]
            return carry

        lax.fori_loop(0, step // 32, widen, 0)

    pool32[POOL * PARTS :, :] = jnp.zeros((2 * PARTS, LANES), F32)

    def pick_seed(b, carry):
        for u in range(8):
            k = b * 8 + u
            where = seed[k]
            away = lax.shift_right_arithmetic(where, 12) - row
            away = jnp.minimum(jnp.maximum(away, -away), 1)
            index = select[jnp.bitwise_and(where, ROWS - 1)]
            index = index + (POOL - index) * away
            seeds32[pl.ds(pl.multiple_of(k * PARTS, PARTS), PARTS), :] = pool32[pl.ds(index * PARTS, PARTS), :]
        return carry

    lax.fori_loop(0, CENT // 8, pick_seed, 0)
    seeds16[...] = seeds32[...].astype(BF16)

    pl.semaphore_wait(barrier, len(partners))

    def reduce_scatter(phase, u, src, core_rx, x_rx, x_tx, z_rx, z_tx):
        dtype = src.dtype
        half = Z * u
        arrived(core_rx, rs_send.at[phase, 0], rs_recv.at[phase, 0], sibling)
        for d in FAR_FIRST + (0,):
            w = (z + d) % Z
            theirs = (1 - xh) * half + w * u
            x_tx[d] = (src[rows(core * 2 * half + theirs, u), :].astype(F32)
                       + core_rx[rows(theirs, u), :].astype(F32)).astype(dtype)
            send(x_tx.at[d], x_rx.at[d], rs_send.at[phase, 1 + d], rs_recv.at[phase, 1 + d], across)
        for d in FAR_FIRST + (0,):
            w = (z + d) % Z
            mine = xh * half + w * u
            arrived(x_rx.at[d], rs_send.at[phase, 1 + d], rs_recv.at[phase, 1 + d], across)
            total = (src[rows(core * 2 * half + mine, u), :].astype(F32)
                     + core_rx[rows(mine, u), :].astype(F32)) + x_rx[d].astype(F32)
            if d:
                z_tx[d] = total.astype(dtype)
                send(z_tx.at[d], z_rx.at[d], rs_send.at[phase, 8 + d], rs_recv.at[phase, 8 + d], z_id(d))
        for d in range(1, Z):
            arrived(z_rx.at[d], rs_send.at[phase, 8 + d], rs_recv.at[phase, 8 + d], z_id(Z - d))
            total = total + z_rx[d].astype(F32)
        return total

    def normalize(v):
        return v * lax.rsqrt(jnp.sum(v * v, axis=1, keepdims=True) + 1e-06)

    def all_gather(phase, dst):
        def part(xh_, z_, core_):
            return dst.at[rows(core_ * 256 + xh_ * 128 + z_ * OWN, OWN)]

        def sems(i):
            return ag_send.at[phase, i], ag_recv.at[phase, i]

        mine = part(xh, z, core)
        for d in FAR_FIRST:
            send(mine, mine, *sems(d), z_id(d))
        send(mine, mine, *sems(8), across)
        send(mine, mine, *sems(16), sibling)
        near_first = FAR_FIRST[::-1]
        for d in near_first:
            block = part(xh, (z - d + Z) % Z, core)
            arrived(block, *sems(d), z_id(Z - d))
            send(block, block, *sems(8 + d), across)
            send(block, block, *sems(16 + d), sibling)
        for d in (0,) + near_first:
            block = part(1 - xh, (z - d + Z) % Z, core)
            arrived(block, *sems(8 + d), across)
            send(block, block, *sems(24 + d), sibling)
        for d in (0,) + near_first:
            arrived(part(xh, (z - d + Z) % Z, 1 - core), *sems(16 + d), sibling)
            arrived(part(1 - xh, (z - d + Z) % Z, 1 - core), *sems(24 + d), sibling)

    u = OWN * PARTS
    send(
        seeds16.at[rows((1 - core) * 16 * u, 16 * u)], core16,
        rs_send.at[0, 0], rs_recv.at[0, 0], sibling,
    )

    def gather(b, carry):
        for v in range(16):
            i = b * 16 + v
            index = select[i]
            sample32[pl.ds(pl.multiple_of(i * PARTS, PARTS), PARTS), :] = pool32[
                pl.ds(index * PARTS, PARTS), :
            ]
        return carry

    lax.fori_loop(0, ROWS // 16, gather, 0)

    def narrow(b, carry):
        start = b * 32
        for t in range(PARTS):
            sample[rows(start, 32), t * LANES : (t + 1) * LANES] = sample32[
                pl.ds(start * PARTS + t, 32, stride=PARTS), :
            ].astype(BF16)
        return carry

    lax.fori_loop(0, ROWS // 32, narrow, 0)

    own32[...] = reduce_scatter(0, u, seeds16, core16, x16, xs16, z16, zs16)
    seeded = jnp.concatenate([own32[pl.ds(t, OWN, stride=PARTS), :] for t in range(PARTS)], axis=1)
    mine = rows(core * 256 + xh * 128 + z * OWN, OWN)
    centers[0, mine, :] = normalize(seeded).astype(BF16)
    all_gather(0, centers.at[0])

    for it in range(2):
        current = centers.at[it]

        def score(j, slot):
            scores[slot] = lax.dot_general(
                current[...], sample[rows(j * BLOCK, BLOCK), :],
                (((1,), (1,)), ((), ())), preferred_element_type=F32,
            )

        def soften(j, slot):
            top = [scores[slot, 8 * i : 8 * i + 8, :] for i in range(2)]
            for i in range(2, CENT // 8):
                top[i % 2] = jnp.maximum(top[i % 2], scores[slot, 8 * i : 8 * i + 8, :])
            top = jnp.max(jnp.maximum(top[0], top[1]), axis=0, keepdims=True)
            total = [jnp.zeros((8, BLOCK), F32)] * 2
            for i in range(CENT // 8):
                e = jnp.exp(scores[slot, 8 * i : 8 * i + 8, :] - top)
                expo[j, 8 * i : 8 * i + 8, :] = e
                total[i % 2] = total[i % 2] + e
            total = jnp.sum(total[0] + total[1], axis=0, keepdims=True)
            g = j // (BLOCKS // GROUPS)
            columns = rows((j % (BLOCKS // GROUPS)) * BLOCK, BLOCK)
            stats[it, g, 0, 0:1, columns] = top
            stats[it, g, 0, 1:2, columns] = total

        score(0, 0)
        for g in range(GROUPS):
            for j in range(g * BLOCKS // GROUPS, (g + 1) * BLOCKS // GROUPS):
                if j + 1 < BLOCKS:
                    score(j + 1, (j + 1) % 2)
                soften(j, j % 2)
            for d in range(1, CENTS):
                send(
                    stats.at[it, g, 0], stats.at[it, g, d],
                    stat_send.at[it, g, d], stat_recv.at[it, g, d], cent_id(d),
                )

        def merge(g):
            for d in range(1, CENTS):
                arrived(
                    stats.at[it, g, d], stat_send.at[it, g, d], stat_recv.at[it, g, d], cent_id(CENTS - d)
                )
            tops = [stats[it, g, d, 0:1, :] for d in range(CENTS)]
            top = tops[0]
            for other in tops[1:]:
                top = jnp.maximum(top, other)
            shares = [jnp.exp(other - top) for other in tops]
            total = shares[0] * stats[it, g, 0, 1:2, :]
            for d in range(1, CENTS):
                total = total + shares[d] * stats[it, g, d, 1:2, :]
            scale[0:1, g * GROUP : (g + 1) * GROUP] = shares[0] / total
            if it == 1:
                energy_out[0:1, g * GROUP : (g + 1) * GROUP] = top + jnp.log(total)

        for first in (True, False):
            start = ((1 - core) if first else core) * 256
            for g in range(GROUPS):
                if first:
                    merge(g)
                per = BLOCKS // GROUPS
                probs = jnp.concatenate(
                    [
                        (expo[j, rows(start, 256), :] * scale[0:1, j * BLOCK : (j + 1) * BLOCK]).astype(BF16)
                        for j in range(g * per, (g + 1) * per)
                    ],
                    axis=1,
                )
                term = jnp.dot(
                    probs, sample[g * GROUP : (g + 1) * GROUP, :], preferred_element_type=F32
                )
                if g:
                    sums[it, rows(start, 256), :] += term
                else:
                    sums[it, rows(start, 256), :] = term
            if first:
                send(
                    sums.at[it, rows(start, 256)], core32.at[it],
                    rs_send.at[1 + it, 0], rs_recv.at[1 + it, 0], sibling,
                )
        total = reduce_scatter(
            1 + it, OWN, sums.at[it], core32.at[it], x32.at[it], xs32.at[it], z32.at[it], zs32.at[it]
        )
        dst = centers.at[1] if it == 0 else centers_out
        dst[mine, :] = normalize(total).astype(BF16)
        all_gather(1 + it, dst)

    for copy in sent:
        copy.wait_send()


def on_device(embedding_pool, select_index, seed_index):
    vmem = pl.BlockSpec(memory_space=pltpu.VMEM)
    smem = pl.BlockSpec(memory_space=pltpu.SMEM)
    u = OWN * PARTS
    centers, energy = pl.pallas_call(
        kernel,
        out_shape=(
            jax.ShapeDtypeStruct((CENT, D), BF16),
            jax.ShapeDtypeStruct((1, ROWS), F32),
        ),
        in_specs=[pl.BlockSpec(memory_space=pl.ANY), smem, smem],
        out_specs=(vmem, vmem),
        scratch_shapes=[
            pltpu.VMEM((POOL, D), BF16),
            pltpu.VMEM(((POOL + 2) * PARTS, LANES), F32),
            pltpu.VMEM((ROWS * PARTS, LANES), F32),
            pltpu.VMEM((ROWS, D), BF16),
            pltpu.VMEM((CENT * PARTS, LANES), F32),
            pltpu.VMEM((BLOCKS, CENT, BLOCK), F32),
            pltpu.VMEM((2, CENT, BLOCK), F32),
            pltpu.VMEM((2, GROUPS, CENTS, 2, GROUP), F32),
            pltpu.VMEM((1, ROWS), F32),
            pltpu.VMEM((2, CENT, D), F32),
            pltpu.VMEM((CENT * PARTS, LANES), BF16),
            pltpu.VMEM((CENT * PARTS // 2, LANES), BF16),
            pltpu.VMEM((Z, u, LANES), BF16),
            pltpu.VMEM((Z, u, LANES), BF16),
            pltpu.VMEM((Z, u, LANES), BF16),
            pltpu.VMEM((Z, u, LANES), BF16),
            pltpu.VMEM((u, LANES), F32),
            pltpu.VMEM((2, CENT // 2, D), F32),
            pltpu.VMEM((2, Z, OWN, D), F32),
            pltpu.VMEM((2, Z, OWN, D), F32),
            pltpu.VMEM((2, Z, OWN, D), F32),
            pltpu.VMEM((2, Z, OWN, D), F32),
            pltpu.VMEM((2, CENT, D), BF16),
            pltpu.SemaphoreType.DMA((LOADS,)),
            pltpu.SemaphoreType.DMA((3, 16)),
            pltpu.SemaphoreType.DMA((3, 16)),
            pltpu.SemaphoreType.DMA((3, 32)),
            pltpu.SemaphoreType.DMA((3, 32)),
            pltpu.SemaphoreType.DMA((2, GROUPS, CENTS)),
            pltpu.SemaphoreType.DMA((2, GROUPS, CENTS)),
        ],
        compiler_params=pltpu.CompilerParams(
            collective_id=0, has_side_effects=True, vmem_limit_bytes=60 * 1024 * 1024
        ),
        cost_estimate=pl.CostEstimate(
            flops=8 * ROWS * CENT * D, bytes_accessed=POOL * D * 2, transcendentals=2 * ROWS * CENT
        ),
    )(embedding_pool, select_index, seed_index)
    return (centers, energy.reshape(ROWS))


def solution(mesh):
    placed = (P("row", None), P("row"), P("cent"))
    return jax.shard_map(
        on_device,
        mesh=mesh,
        in_specs=placed,
        out_specs=(P("cent", None), P("row")),
        check_vma=False,
    )
```

```python
import jax
import jax.numpy as jnp
from jax import lax
from jax.experimental import pallas as pl
from jax.experimental.pallas import tpu as pltpu
from jax.sharding import PartitionSpec as P

F32 = jnp.float32
BF16 = jnp.bfloat16
MESH = pl.DeviceIdType.MESH

POOL = 8192
ROWS = 4096
CENT = 512
HALF = CENT // 2
D = 512
LANES = 128
PARTS = D // LANES
LOADS = 16
BLOCK = 512
BLOCKS = ROWS // BLOCK
GROUPS = ((0, 2), (2, 4), (4, 7), (7, 8))
GROUP = 3 * BLOCK
OWN = 16
Z = 8
CENTS = 8
FAR_FIRST = (4, 3, 5, 2, 6, 1, 7)
NEAR_FIRST = FAR_FIRST[::-1]


def rows(start, size):
    return pl.ds(pl.multiple_of(start, size), size)


def normalize(v):
    return v * lax.rsqrt(jnp.sum(v * v, axis=1, keepdims=True) + 1e-06)


def pack(v):
    top = jnp.maximum(jnp.max(jnp.abs(v), axis=1, keepdims=True), 1e-30)
    exponent = jnp.ceil(jnp.log2(top))
    coded = jnp.round(v * (jnp.exp2(15.0 - exponent) * 0.999)).astype(jnp.int32)
    exponent = jnp.broadcast_to(exponent, (v.shape[0], LANES)).astype(jnp.int32)
    return jnp.concatenate([coded, exponent], axis=1).astype(jnp.int16)


def unpack(w):
    w = w.astype(jnp.int32).astype(F32)
    unit = jnp.exp2(w[:, D:] - 15.0) * (1.0 / 0.999)
    return jnp.concatenate([w[:, t * LANES : (t + 1) * LANES] * unit for t in range(PARTS)], axis=1)


def kernel(
    pool_hbm,
    select,
    seed,
    centers_out,
    energy_out,
    pool_in,
    pool32,
    sample32,
    sample,
    seeds32,
    expo,
    scores,
    local,
    stats,
    scale,
    sums,
    seeds16,
    core16,
    core32,
    own32,
    x_rx0,
    x_tx0,
    z_rx0,
    z_tx0,
    x_rx,
    x_tx,
    z_rx,
    z_tx,
    centers,
    load_sem,
    rs_send,
    rs_recv,
    ag_send,
    ag_recv,
    stat_send,
    stat_recv,
):
    row = lax.axis_index("row")
    cent = lax.axis_index("cent")
    xh = row // 16
    z = (row // 2) % Z
    core = row % 2

    def row_id(xh_, z_, core_):
        return xh_ * 16 + z_ * 2 + core_

    sibling = (row_id(xh, z, 1 - core), cent)
    across = (row_id(1 - xh, z, core), cent)

    def z_id(distance):
        return (row_id(xh, (z + distance) % Z, core), cent)

    def cent_id(distance):
        return (row, (cent + distance) % CENTS)

    sent = []

    def send(src, dst, send_sem, recv_sem, device):
        copy = pltpu.make_async_remote_copy(
            src_ref=src, dst_ref=dst, send_sem=send_sem, recv_sem=recv_sem,
            device_id=device, device_id_type=MESH,
        )
        copy.start()
        sent.append(copy)

    def drain():
        for copy in sent:
            copy.wait_send()
        sent.clear()

    def arrived(dst, send_sem, recv_sem, device):
        pltpu.make_async_remote_copy(
            src_ref=dst, dst_ref=dst, send_sem=send_sem, recv_sem=recv_sem,
            device_id=device, device_id_type=MESH,
        ).wait_recv()

    step = POOL // LOADS

    def load(i):
        part = rows(i * step, step)
        return pltpu.make_async_copy(pool_hbm.at[part], pool_in.at[part], load_sem.at[i])

    for i in range(LOADS):
        load(i).start()
    barrier = pltpu.get_barrier_semaphore()
    partners = [sibling, across] + [z_id(d) for d in range(1, Z)] + [cent_id(d) for d in range(1, CENTS)]
    for partner in partners:
        pl.semaphore_signal(barrier, inc=1, device_id=partner, device_id_type=MESH)

    def widen(i, carry):
        load(i).wait()
        for b in range(step // 128):
            start = pl.multiple_of(i * step + b * 128, 128)
            block = pool_in[pl.ds(start, 128), :].astype(F32)
            for t in range(PARTS):
                pool32[pl.ds(start * PARTS + t, 128, stride=PARTS), :] = block[:, t * LANES : (t + 1) * LANES]
        return carry

    lax.fori_loop(0, LOADS, widen, 0)
    pool32[POOL * PARTS :, :] = jnp.zeros((2 * PARTS, LANES), F32)

    def pick_seed(b, carry):
        for v in range(16):
            k = b * 16 + v
            where = seed[k]
            away = lax.shift_right_arithmetic(where, 12) - row
            away = jnp.minimum(jnp.maximum(away, -away), 1)
            index = select[jnp.bitwise_and(where, ROWS - 1)]
            index = index + (POOL - index) * away
            seeds32[pl.ds(pl.multiple_of(k * PARTS, PARTS), PARTS), :] = pool32[pl.ds(index * PARTS, PARTS), :]
        return carry

    lax.fori_loop(0, CENT // 16, pick_seed, 0)
    seeds16[...] = seeds32[...].astype(BF16)

    def gather(b, carry):
        for v in range(64):
            i = b * 64 + v
            index = select[i]
            sample32[pl.ds(pl.multiple_of(i * PARTS, PARTS), PARTS), :] = pool32[pl.ds(index * PARTS, PARTS), :]
        return carry

    def narrow(b, carry):
        start = b * 128
        for t in range(PARTS):
            sample[rows(start, 128), t * LANES : (t + 1) * LANES] = sample32[
                pl.ds(start * PARTS + t, 128, stride=PARTS), :
            ].astype(BF16)
        return carry

    def core_sems(phase, other):
        return rs_send.at[phase, 16 + other], rs_recv.at[phase, 16 + other]

    def reduce_scatter(phase, own, other, core_rx, x_rx, x_tx, z_rx, z_tx, code, decode, beside_x=None, beside_z=None):
        u = x_rx.shape[1]

        def sems(i):
            return rs_send.at[phase, i], rs_recv.at[phase, i]

        arrived(core_rx.at[1], *core_sems(phase, 1), sibling)
        for d in FAR_FIRST + (0,):
            w = (z + d) % Z
            x_tx[d] = code(other(w) + core_rx[1, rows(w * u, u), :].astype(F32))
            send(x_tx.at[d], x_rx.at[d], *sems(d), across)
        if beside_x:
            beside_x()
        arrived(core_rx.at[0], *core_sems(phase, 0), sibling)
        for d in FAR_FIRST + (0,):
            w = (z + d) % Z
            arrived(x_rx.at[d], *sems(d), across)
            total = (own(w) + core_rx[0, rows(w * u, u), :].astype(F32)) + decode(x_rx[d])
            if d:
                z_tx[d] = code(total)
                send(z_tx.at[d], z_rx.at[d], *sems(8 + d), z_id(d))
        if beside_z:
            beside_z()
        for d in NEAR_FIRST:
            arrived(z_rx.at[d], *sems(8 + d), z_id(Z - d))
            total = total + decode(z_rx[d])
        return total

    def part(dst, xh_, z_, core_):
        return dst.at[rows(xh_ * HALF + core_ * (Z * OWN) + z_ * OWN, OWN)]

    def ag_sems(phase, i):
        return ag_send.at[phase, i], ag_recv.at[phase, i]

    def gather_near(phase, dst, beside=None):
        mine = part(dst, xh, z, core)
        for d in FAR_FIRST:
            send(mine, mine, *ag_sems(phase, d), z_id(d))
        send(mine, mine, *ag_sems(phase, 8), across)
        send(mine, mine, *ag_sems(phase, 16), sibling)
        if beside:
            beside()
        for d in NEAR_FIRST:
            block = part(dst, xh, (z - d + Z) % Z, core)
            arrived(block, *ag_sems(phase, d), z_id(Z - d))
            send(block, block, *ag_sems(phase, 8 + d), across)
            send(block, block, *ag_sems(phase, 16 + d), sibling)
        for d in (0,) + NEAR_FIRST:
            arrived(part(dst, xh, (z - d + Z) % Z, 1 - core), *ag_sems(phase, 16 + d), sibling)

    def pass_on(phase, dst, i):
        d = ((0,) + NEAR_FIRST)[i]
        block = part(dst, 1 - xh, (z - d + Z) % Z, core)
        arrived(block, *ag_sems(phase, 8 + d), across)
        send(block, block, *ag_sems(phase, 24 + d), sibling)

    def gather_far(phase, dst):
        for d in (0,) + NEAR_FIRST:
            arrived(part(dst, 1 - xh, (z - d + Z) % Z, 1 - core), *ag_sems(phase, 24 + d), sibling)

    u = OWN * PARTS
    pl.semaphore_wait(barrier, len(partners))
    for other in (1, 0):
        side = (1 - xh) if other else xh
        send(
            seeds16.at[rows((side * 2 + 1 - core) * Z * u, Z * u)], core16.at[other],
            *core_sems(0, other), sibling,
        )

    def seeds_of(side):
        return lambda w: seeds16[rows((side * 2 + core) * Z * u + w * u, u), :].astype(F32)

    own32[...] = reduce_scatter(
        0, seeds_of(xh), seeds_of(1 - xh), core16, x_rx0, x_tx0, z_rx0, z_tx0,
        lambda v: v.astype(BF16), lambda v: v.astype(F32),
        lambda: lax.fori_loop(0, ROWS // 128, gather, 0),
        lambda: lax.fori_loop(ROWS // 128, ROWS // 64, gather, 0),
    )
    seeded = jnp.concatenate([own32[pl.ds(t, OWN, stride=PARTS), :] for t in range(PARTS)], axis=1)
    mine = rows(xh * HALF + core * (Z * OWN) + z * OWN, OWN)
    centers[0, mine, :] = normalize(seeded).astype(BF16)
    gather_near(0, centers.at[0], lambda: lax.fori_loop(0, ROWS // 128, narrow, 0))

    for it in range(2):
        current = centers.at[it]

        def stats_of(g, d):
            first, last = GROUPS[g]
            return stats.at[it, g, d, :, pl.ds(0, (last - first) * BLOCK)]

        def score(side, j):
            start = (xh if side == 0 else 1 - xh) * HALF
            scores[j % 2] = lax.dot_general(
                current[rows(start, HALF), :], sample[j * BLOCK : (j + 1) * BLOCK, :],
                (((1,), (1,)), ((), ())), preferred_element_type=F32,
            )

        def soften(side, j):
            slot = j % 2
            top = [scores[slot, 8 * i : 8 * i + 8, :] for i in range(2)]
            for i in range(2, HALF // 8):
                top[i % 2] = jnp.maximum(top[i % 2], scores[slot, 8 * i : 8 * i + 8, :])
            top = jnp.max(jnp.maximum(top[0], top[1]), axis=0, keepdims=True)
            total = [jnp.zeros((8, BLOCK), F32)] * 2
            for i in range(HALF // 8):
                e = jnp.exp(scores[slot, 8 * i : 8 * i + 8, :] - top)
                expo[side, j, 8 * i : 8 * i + 8, :] = e
                total[i % 2] = total[i % 2] + e
            total = jnp.sum(total[0] + total[1], axis=0, keepdims=True)
            columns = slice(j * BLOCK, (j + 1) * BLOCK)
            local[side, 0:1, columns] = top
            if side == 0:
                local[0, 1:2, columns] = total
            else:
                near = local[0, 0:1, columns]
                both = jnp.maximum(near, top)
                total = total * jnp.exp(top - both) + local[0, 1:2, columns] * jnp.exp(near - both)
                g = [first <= j < last for first, last in GROUPS].index(True)
                inside = slice((j - GROUPS[g][0]) * BLOCK, (j - GROUPS[g][0] + 1) * BLOCK)
                stats[it, g, 0, 0:1, inside] = both
                stats[it, g, 0, 1:2, inside] = total

        for side in (0, 1):
            if side:
                gather_far(it, current)
            score(side, 0)
            for j in range(BLOCKS):
                if j + 1 < BLOCKS:
                    score(side, j + 1)
                soften(side, j)
                if side == 0:
                    pass_on(it, current, j)
                elif j + 1 in [last for _, last in GROUPS]:
                    g = [last for _, last in GROUPS].index(j + 1)
                    for d in range(1, CENTS):
                        send(
                            stats_of(g, 0), stats_of(g, d),
                            stat_send.at[it, g, d], stat_recv.at[it, g, d], cent_id(d),
                        )

        def merge(g):
            for d in range(1, CENTS):
                arrived(
                    stats_of(g, d), stat_send.at[it, g, d], stat_recv.at[it, g, d], cent_id(CENTS - d)
                )
            first, last = GROUPS[g]
            size = (last - first) * BLOCK
            tops = [stats[it, g, d, 0:1, 0:size] for d in range(CENTS)]
            top = tops[0]
            for other in tops[1:]:
                top = jnp.maximum(top, other)
            total = jnp.exp(tops[0] - top) * stats[it, g, 0, 1:2, 0:size]
            for d in range(1, CENTS):
                total = total + jnp.exp(tops[d] - top) * stats[it, g, d, 1:2, 0:size]
            columns = slice(first * BLOCK, last * BLOCK)
            for side in range(2):
                scale[side, 0:1, columns] = jnp.exp(local[side, 0:1, columns] - top) / total
            if it == 1:
                energy_out[0:1, columns] = top + jnp.log(total)

        def add_up(side, g):
            probs = jnp.concatenate(
                [
                    (expo[side, j] * scale[side, 0:1, j * BLOCK : (j + 1) * BLOCK]).astype(BF16)
                    for j in range(*GROUPS[g])
                ],
                axis=1,
            )
            term = jnp.dot(probs, sample[GROUPS[g][0] * BLOCK : GROUPS[g][1] * BLOCK, :], preferred_element_type=F32)
            if g:
                sums[it, side] += term
            else:
                sums[it, side] = term

        def exchange(other):
            send(
                sums.at[it, other, rows((1 - core) * Z * OWN, Z * OWN)], core32.at[it, other],
                *core_sems(1 + it, other), sibling,
            )

        def sums_of(side):
            return lambda w: sums[it, side, rows(core * Z * OWN + w * OWN, OWN), :]

        for g in range(len(GROUPS)):
            merge(g)
            for side in (1, 0):
                add_up(side, g)
                if g == len(GROUPS) - 1:
                    exchange(side)
        total = reduce_scatter(
            1 + it, sums_of(0), sums_of(1), core32.at[it],
            x_rx.at[it], x_tx.at[it], z_rx.at[it], z_tx.at[it], pack, unpack, None, drain,
        )
        dst = centers.at[1] if it == 0 else centers_out
        dst[mine, :] = normalize(total).astype(BF16)
        gather_near(1 + it, dst)
    for i in range(Z):
        pass_on(2, centers_out, i)
    drain()
    gather_far(2, centers_out)


def hand_on(centers_in, energy_in, centers_out, energy_out):
    centers_out[...] = centers_in[...]
    energy_out[...] = energy_in[...]


def on_device(embedding_pool, select_index, seed_index):
    vmem = pl.BlockSpec(memory_space=pltpu.VMEM)
    smem = pl.BlockSpec(memory_space=pltpu.SMEM)
    u = OWN * PARTS
    seed_slots = pltpu.VMEM((Z, u, LANES), BF16)
    slots = pltpu.VMEM((2, Z, OWN, D + LANES), jnp.int16)
    centers, energy = pl.pallas_call(
        kernel,
        out_shape=(
            jax.ShapeDtypeStruct((CENT, D), BF16),
            jax.ShapeDtypeStruct((1, ROWS), F32),
        ),
        in_specs=[pl.BlockSpec(memory_space=pl.ANY), smem, smem],
        out_specs=(vmem, vmem),
        scratch_shapes=[
            pltpu.VMEM((POOL, D), BF16),
            pltpu.VMEM(((POOL + 2) * PARTS, LANES), F32),
            pltpu.VMEM((ROWS * PARTS, LANES), F32),
            pltpu.VMEM((ROWS, D), BF16),
            pltpu.VMEM((CENT * PARTS, LANES), F32),
            pltpu.VMEM((2, BLOCKS, HALF, BLOCK), F32),
            pltpu.VMEM((2, HALF, BLOCK), F32),
            pltpu.VMEM((2, 2, ROWS), F32),
            pltpu.VMEM((2, len(GROUPS), CENTS, 2, GROUP), F32),
            pltpu.VMEM((2, 1, ROWS), F32),
            pltpu.VMEM((2, 2, HALF, D), F32),
            pltpu.VMEM((CENT * PARTS, LANES), BF16),
            pltpu.VMEM((2, Z * u, LANES), BF16),
            pltpu.VMEM((2, 2, Z * OWN, D), F32),
            pltpu.VMEM((u, LANES), F32),
            seed_slots, seed_slots, seed_slots, seed_slots,
            slots, slots, slots, slots,
            pltpu.VMEM((2, CENT, D), BF16),
            pltpu.SemaphoreType.DMA((LOADS,)),
            pltpu.SemaphoreType.DMA((3, 18)),
            pltpu.SemaphoreType.DMA((3, 18)),
            pltpu.SemaphoreType.DMA((3, 32)),
            pltpu.SemaphoreType.DMA((3, 32)),
            pltpu.SemaphoreType.DMA((2, len(GROUPS), CENTS)),
            pltpu.SemaphoreType.DMA((2, len(GROUPS), CENTS)),
        ],
        compiler_params=pltpu.CompilerParams(
            collective_id=0, has_side_effects=True, vmem_limit_bytes=60 * 1024 * 1024
        ),
        cost_estimate=pl.CostEstimate(
            flops=8 * ROWS * CENT * D, bytes_accessed=POOL * D * 2, transcendentals=2 * ROWS * CENT
        ),
    )(embedding_pool, select_index, seed_index)
    return pl.pallas_call(
        hand_on,
        out_shape=(
            jax.ShapeDtypeStruct((CENT, D), BF16),
            jax.ShapeDtypeStruct((ROWS,), F32),
        ),
        in_specs=[vmem, vmem],
        out_specs=(vmem, vmem),
        cost_estimate=pl.CostEstimate(flops=0, bytes_accessed=4 * CENT * D + 8 * ROWS, transcendentals=0),
    )(centers, energy.reshape(ROWS))


def solution(mesh):
    placed = (P("row", None), P("row"), P("cent"))
    return jax.shard_map(
        on_device,
        mesh=mesh,
        in_specs=placed,
        out_specs=(P("cent", None), P("row")),
        check_vma=False,
    )
```

```python
import jax
import jax.numpy as jnp
from jax import lax
from jax.experimental import pallas as pl
from jax.experimental.pallas import tpu as pltpu
from jax.sharding import PartitionSpec as P

F32 = jnp.float32
BF16 = jnp.bfloat16
MESH = pl.DeviceIdType.MESH

POOL = 8192
ROWS = 4096
CENT = 512
CHIP_ROWS = 2 * ROWS
HALF = CENT // 4
D = 512
LANES = 128
PARTS = D // LANES
LOADS = 16
BLOCK = 1024
BLOCKS = CHIP_ROWS // BLOCK
PIECE = 1024
GROUPS = ((0, 2), (2, 4), (4, 7), (7, 8))
GROUP = 3 * BLOCK
JOINS = {4: (0,), 6: (1,), 7: (2, 3)}
OWN = 16
Z = 8
CENTS = 8
FAR_FIRST = (4, 3, 5, 2, 6, 1, 7)
NEAR_FIRST = FAR_FIRST[::-1]


def rows(start, size):
    return pl.ds(pl.multiple_of(start, size), size)


def log_sum(logs):
    top = logs[0]
    for other in logs[1:]:
        top = jnp.maximum(top, other)
    total = jnp.exp(logs[0] - top)
    for other in logs[1:]:
        total = total + jnp.exp(other - top)
    return top + jnp.log(total)


def normalize(v):
    return v * lax.rsqrt(jnp.sum(v * v, axis=1, keepdims=True) + 1e-06)


def pack(v):
    top = jnp.maximum(jnp.max(jnp.abs(v), axis=1, keepdims=True), 1e-30)
    exponent = jnp.ceil(jnp.log2(top))
    coded = jnp.round(v * (jnp.exp2(15.0 - exponent) * 0.999)).astype(jnp.int32)
    exponent = jnp.broadcast_to(exponent, (v.shape[0], LANES)).astype(jnp.int32)
    return jnp.concatenate([coded, exponent], axis=1).astype(jnp.int16)


def unpack(w):
    w = w.astype(jnp.int32).astype(F32)
    unit = jnp.exp2(w[:, D:] - 15.0) * (1.0 / 0.999)
    return jnp.concatenate([w[:, t * LANES : (t + 1) * LANES] * unit for t in range(PARTS)], axis=1)


def kernel(
    pool_hbm,
    select,
    seed,
    centers_out,
    energy_out,
    pool_in,
    pool32,
    sample32,
    sample,
    seeds32,
    expo,
    scores,
    local,
    pair,
    stats,
    scale,
    sums,
    seeds16,
    core16,
    energy,
    own32,
    x_rx0,
    x_tx0,
    z_rx0,
    z_tx0,
    x_rx,
    x_tx,
    z_rx,
    z_tx,
    centers,
    load_sem,
    rs_send,
    rs_recv,
    ag_send,
    ag_recv,
    stat_send,
    stat_recv,
    pair_send,
    pair_recv,
    sample_send,
    sample_recv,
):
    row = lax.axis_index("row")
    cent = lax.axis_index("cent")
    xh = row // 16
    z = (row // 2) % Z
    core = row % 2

    def row_id(xh_, z_, core_):
        return xh_ * 16 + z_ * 2 + core_

    sibling = (row_id(xh, z, 1 - core), cent)
    across = (row_id(1 - xh, z, core), cent)

    def z_id(distance):
        return (row_id(xh, (z + distance) % Z, core), cent)

    def cent_id(distance):
        return (row, (cent + distance) % CENTS)

    sent = []

    def send(src, dst, send_sem, recv_sem, device):
        copy = pltpu.make_async_remote_copy(
            src_ref=src, dst_ref=dst, send_sem=send_sem, recv_sem=recv_sem,
            device_id=device, device_id_type=MESH,
        )
        copy.start()
        sent.append(copy)

    def drain():
        for copy in sent:
            copy.wait_send()
        sent.clear()

    def arrived(dst, send_sem, recv_sem, device):
        pltpu.make_async_remote_copy(
            src_ref=dst, dst_ref=dst, send_sem=send_sem, recv_sem=recv_sem,
            device_id=device, device_id_type=MESH,
        ).wait_recv()

    step = POOL // LOADS

    def load(i):
        part = rows(i * step, step)
        return pltpu.make_async_copy(pool_hbm.at[part], pool_in.at[part], load_sem.at[i])

    for i in range(LOADS):
        load(i).start()
    barrier = pltpu.get_barrier_semaphore()
    partners = [sibling, across] + [z_id(d) for d in range(1, Z)] + [cent_id(d) for d in range(1, CENTS)]
    for partner in partners:
        pl.semaphore_signal(barrier, inc=1, device_id=partner, device_id_type=MESH)

    def widen(i, carry):
        load(i).wait()
        for b in range(step // 128):
            start = pl.multiple_of(i * step + b * 128, 128)
            block = pool_in[pl.ds(start, 128), :].astype(F32)
            for t in range(PARTS):
                pool32[pl.ds(start * PARTS + t, 128, stride=PARTS), :] = block[:, t * LANES : (t + 1) * LANES]
        return carry

    lax.fori_loop(0, LOADS, widen, 0)
    pool32[POOL * PARTS :, :] = jnp.zeros((2 * PARTS, LANES), F32)

    def pick_seed(b, carry):
        for v in range(16):
            k = b * 16 + v
            where = seed[k]
            away = lax.shift_right_arithmetic(where, 12) - row
            away = jnp.minimum(jnp.maximum(away, -away), 1)
            index = select[jnp.bitwise_and(where, ROWS - 1)]
            index = index + (POOL - index) * away
            seeds32[pl.ds(pl.multiple_of(k * PARTS, PARTS), PARTS), :] = pool32[pl.ds(index * PARTS, PARTS), :]
        return carry

    lax.fori_loop(0, CENT // 16, pick_seed, 0)
    seeds16[...] = seeds32[...].astype(BF16)

    def gather_piece(p):
        def gather(b, carry):
            for v in range(64):
                i = b * 64 + v
                index = select[p * PIECE + i]
                sample32[pl.ds(pl.multiple_of(i * PARTS, PARTS), PARTS), :] = pool32[
                    pl.ds(index * PARTS, PARTS), :
                ]
            return carry

        def narrow(b, carry):
            start = b * 128
            for t in range(PARTS):
                sample[rows(core * ROWS + p * PIECE + start, 128), t * LANES : (t + 1) * LANES] = sample32[
                    pl.ds(start * PARTS + t, 128, stride=PARTS), :
                ].astype(BF16)
            return carry

        lax.fori_loop(0, PIECE // 64, gather, 0)
        lax.fori_loop(0, PIECE // 128, narrow, 0)

    def gather_pieces(first, last):
        for p in range(first, last):
            gather_piece(p)

    def share_samples():
        for p in range(ROWS // PIECE):
            piece = sample.at[rows(core * ROWS + p * PIECE, PIECE)]
            send(piece, piece, sample_send.at[p], sample_recv.at[p], sibling)

    def beside_z():
        gather_pieces(2, 4)
        share_samples()

    def core_sems(phase, other):
        return rs_send.at[phase, 16 + other], rs_recv.at[phase, 16 + other]

    def reduce_scatter(phase, own, other, x_rx, x_tx, z_rx, z_tx, code, decode, beside_x=None, beside_z=None):
        def sems(i):
            return rs_send.at[phase, i], rs_recv.at[phase, i]

        u = x_rx.shape[1]
        x_tx[...] = code(other)
        for d in FAR_FIRST + (0,):
            send(x_tx.at[rows((z + d) % Z * u, u)], x_rx.at[d], *sems(d), across)
        if beside_x:
            beside_x()
        for d in FAR_FIRST + (0,):
            arrived(x_rx.at[d], *sems(d), across)
            total = own((z + d) % Z) + decode(x_rx[d])
            if d:
                z_tx[d] = code(total)
                send(z_tx.at[d], z_rx.at[d], *sems(8 + d), z_id(d))
        if beside_z:
            beside_z()
        for d in NEAR_FIRST:
            arrived(z_rx.at[d], *sems(8 + d), z_id(Z - d))
            total = total + decode(z_rx[d])
        return total

    def part(dst, xh_, z_, core_):
        return dst.at[rows(xh_ * (2 * HALF) + core_ * HALF + z_ * OWN, OWN)]

    def ag_sems(phase, i):
        return ag_send.at[phase, i], ag_recv.at[phase, i]

    def scored(dst, side, d):
        return dst.at[rows(side * HALF + (z - d + Z) % Z * OWN, OWN)]

    def spread_near(phase, dst):
        mine = scored(dst, 0, 0)
        for d in FAR_FIRST:
            send(mine, mine, *ag_sems(phase, d), z_id(d))
        send(mine, scored(dst, 1, 0), *ag_sems(phase, 8), across)
        for d in NEAR_FIRST:
            block = scored(dst, 0, d)
            arrived(block, *ag_sems(phase, d), z_id(Z - d))
            send(block, scored(dst, 1, d), *ag_sems(phase, 8 + d), across)

    def spread_far(phase, dst):
        for d in (0,) + NEAR_FIRST:
            arrived(scored(dst, 1, d), *ag_sems(phase, 8 + d), across)

    def gather_near(phase, dst, beside=None):
        mine = part(dst, xh, z, core)
        for d in FAR_FIRST:
            send(mine, mine, *ag_sems(phase, d), z_id(d))
        send(mine, mine, *ag_sems(phase, 8), across)
        send(mine, mine, *ag_sems(phase, 16), sibling)
        if beside:
            beside()
        for d in NEAR_FIRST:
            block = part(dst, xh, (z - d + Z) % Z, core)
            arrived(block, *ag_sems(phase, d), z_id(Z - d))
            send(block, block, *ag_sems(phase, 8 + d), across)
            send(block, block, *ag_sems(phase, 16 + d), sibling)
        for d in (0,) + NEAR_FIRST:
            arrived(part(dst, xh, (z - d + Z) % Z, 1 - core), *ag_sems(phase, 16 + d), sibling)

    def pass_on(phase, dst, i):
        d = ((0,) + NEAR_FIRST)[i]
        block = part(dst, 1 - xh, (z - d + Z) % Z, core)
        arrived(block, *ag_sems(phase, 8 + d), across)
        send(block, block, *ag_sems(phase, 24 + d), sibling)

    def gather_far(phase, dst):
        for d in (0,) + NEAR_FIRST:
            arrived(part(dst, 1 - xh, (z - d + Z) % Z, 1 - core), *ag_sems(phase, 24 + d), sibling)

    u = OWN * PARTS
    pl.semaphore_wait(barrier, len(partners))
    for other in (1, 0):
        side = (1 - xh) if other else xh
        send(
            seeds16.at[rows((side * 2 + 1 - core) * Z * u, Z * u)], core16.at[other],
            *core_sems(0, other), sibling,
        )

    arrived(core16.at[1], *core_sems(0, 1), sibling)

    def beside_x():
        gather_pieces(0, 2)
        arrived(core16.at[0], *core_sems(0, 0), sibling)

    def own_seeds(w):
        return (seeds16[rows((xh * 2 + core) * Z * u + w * u, u), :].astype(F32)
                + core16[0, rows(w * u, u), :].astype(F32))

    other_seeds = seeds16[rows(((1 - xh) * 2 + core) * Z * u, Z * u), :].astype(F32) + core16[1].astype(F32)

    own32[...] = reduce_scatter(
        0, own_seeds, other_seeds, x_rx0, x_tx0, z_rx0, z_tx0,
        lambda v: v.astype(BF16), lambda v: v.astype(F32),
        beside_x, beside_z,
    )
    seeded = jnp.concatenate([own32[pl.ds(t, OWN, stride=PARTS), :] for t in range(PARTS)], axis=1)
    centers[0, rows(z * OWN, OWN), :] = normalize(seeded).astype(BF16)
    spread_near(0, centers.at[0])
    for p in range(ROWS // PIECE):
        arrived(
            sample.at[rows((1 - core) * ROWS + p * PIECE, PIECE)], sample_send.at[p], sample_recv.at[p], sibling
        )

    for it in range(2):
        current = centers.at[it]

        def stats_of(g, d):
            first, last = GROUPS[g]
            return stats.at[it, g, d, :, pl.ds(0, (last - first) * BLOCK)]

        def score(side, j):
            scores[j % 2] = lax.dot_general(
                current[side * HALF : (side + 1) * HALF, :], sample[j * BLOCK : (j + 1) * BLOCK, :],
                (((1,), (1,)), ((), ())), preferred_element_type=F32,
            )

        def soften(side, j):
            slot = j % 2
            top = [scores[slot, 8 * i : 8 * i + 8, :] for i in range(2)]
            for i in range(2, HALF // 8):
                top[i % 2] = jnp.maximum(top[i % 2], scores[slot, 8 * i : 8 * i + 8, :])
            top = jnp.max(jnp.maximum(top[0], top[1]), axis=0, keepdims=True)
            total = [jnp.zeros((8, BLOCK), F32)] * 2
            for i in range(HALF // 8):
                e = jnp.exp(scores[slot, 8 * i : 8 * i + 8, :] - top)
                expo[j, side * HALF + 8 * i : side * HALF + 8 * i + 8, :] = e
                total[i % 2] = total[i % 2] + e
            total = jnp.sum(total[0] + total[1], axis=0, keepdims=True)
            columns = slice(j * BLOCK, (j + 1) * BLOCK)
            local[side, 0:1, columns] = top
            if side == 0:
                local[0, 1:2, columns] = total
            else:
                near = local[0, 0:1, columns]
                both = jnp.maximum(near, top)
                total = total * jnp.exp(top - both) + local[0, 1:2, columns] * jnp.exp(near - both)
                g = [first <= j < last for first, last in GROUPS].index(True)
                inside = slice((j - GROUPS[g][0]) * BLOCK, (j - GROUPS[g][0] + 1) * BLOCK)
                pair[it, g, 0, 0:1, inside] = both + jnp.log(total)

        def pair_of(g, c):
            first, last = GROUPS[g]
            return pair.at[it, g, c, :, pl.ds(0, (last - first) * BLOCK)]

        def join(g):
            arrived(pair_of(g, 1), pair_send.at[it, g], pair_recv.at[it, g], sibling)
            inside = slice(0, (GROUPS[g][1] - GROUPS[g][0]) * BLOCK)
            stats[it, g, 0, 0:1, inside] = log_sum([pair[it, g, c, 0:1, inside] for c in range(2)])
            for d in range(1, CENTS):
                send(stats_of(g, 0), stats_of(g, d), stat_send.at[it, g, d], stat_recv.at[it, g, d], cent_id(d))

        for side in (0, 1):
            if side:
                spread_far(it, current)
            score(side, 0)
            for j in range(BLOCKS):
                if j + 1 < BLOCKS:
                    score(side, j + 1)
                soften(side, j)
                if side and j + 1 in [last for _, last in GROUPS]:
                    g = [last for _, last in GROUPS].index(j + 1)
                    send(pair_of(g, 0), pair_of(g, 1), pair_send.at[it, g], pair_recv.at[it, g], sibling)
                if side:
                    for g in JOINS.get(j, ()):
                        join(g)

        def merge(g):
            for d in range(1, CENTS):
                arrived(
                    stats_of(g, d), stat_send.at[it, g, d], stat_recv.at[it, g, d], cent_id(CENTS - d)
                )
            first, last = GROUPS[g]
            size = (last - first) * BLOCK
            total = log_sum([stats[it, g, d, 0:1, 0:size] for d in range(CENTS)])
            columns = slice(first * BLOCK, last * BLOCK)
            for side in range(2):
                scale[side, 0:1, columns] = jnp.exp(local[side, 0:1, columns] - total)
            if it == 1:
                energy[0:1, columns] = total

        def add_up(g):
            probs = jnp.concatenate(
                [
                    jnp.concatenate(
                        [
                            (expo[j, side * HALF : (side + 1) * HALF, :]
                             * scale[side, 0:1, j * BLOCK : (j + 1) * BLOCK]).astype(BF16)
                            for side in range(2)
                        ],
                        axis=0,
                    )
                    for j in range(*GROUPS[g])
                ],
                axis=1,
            )
            term = jnp.dot(
                probs, sample[GROUPS[g][0] * BLOCK : GROUPS[g][1] * BLOCK, :], preferred_element_type=F32
            )
            if g:
                sums[it] += term
            else:
                sums[it] = term

        def own_sums(w):
            return sums[it, rows(w * OWN, OWN), :]

        for g in range(len(GROUPS)):
            merge(g)
            add_up(g)
        total = reduce_scatter(
            1 + it, own_sums, sums[it, HALF:, :],
            x_rx.at[it], x_tx.at[it], z_rx.at[it], z_tx.at[it], pack, unpack, None, drain,
        )
        if it == 0:
            centers[1, rows(z * OWN, OWN), :] = normalize(total).astype(BF16)
            spread_near(1, centers.at[1])
    mine = rows(xh * (2 * HALF) + core * HALF + z * OWN, OWN)
    centers_out[mine, :] = normalize(total).astype(BF16)
    energy_out[...] = energy[:, rows(core * ROWS, ROWS)]
    gather_near(2, centers_out)
    for i in range(Z):
        pass_on(2, centers_out, i)
    drain()
    gather_far(2, centers_out)


def hand_on(centers_in, energy_in, centers_out, energy_out):
    centers_out[...] = centers_in[...]
    energy_out[...] = energy_in[...]


def on_device(embedding_pool, select_index, seed_index):
    vmem = pl.BlockSpec(memory_space=pltpu.VMEM)
    smem = pl.BlockSpec(memory_space=pltpu.SMEM)
    u = OWN * PARTS
    seed_slots = pltpu.VMEM((Z, u, LANES), BF16)
    slots = pltpu.VMEM((2, Z, OWN, D + LANES), jnp.int16)
    centers, energy = pl.pallas_call(
        kernel,
        out_shape=(
            jax.ShapeDtypeStruct((CENT, D), BF16),
            jax.ShapeDtypeStruct((1, ROWS), F32),
        ),
        in_specs=[pl.BlockSpec(memory_space=pl.ANY), smem, smem],
        out_specs=(vmem, vmem),
        scratch_shapes=[
            pltpu.VMEM((POOL, D), BF16),
            pltpu.VMEM(((POOL + 2) * PARTS, LANES), F32),
            pltpu.VMEM((PIECE * PARTS, LANES), F32),
            pltpu.VMEM((CHIP_ROWS, D), BF16),
            pltpu.VMEM((CENT * PARTS, LANES), F32),
            pltpu.VMEM((BLOCKS, 2 * HALF, BLOCK), F32),
            pltpu.VMEM((2, HALF, BLOCK), F32),
            pltpu.VMEM((2, 2, CHIP_ROWS), F32),
            pltpu.VMEM((2, len(GROUPS), 2, 1, GROUP), F32),
            pltpu.VMEM((2, len(GROUPS), CENTS, 1, GROUP), F32),
            pltpu.VMEM((2, 1, CHIP_ROWS), F32),
            pltpu.VMEM((2, 2 * HALF, D), F32),
            pltpu.VMEM((CENT * PARTS, LANES), BF16),
            pltpu.VMEM((2, Z * u, LANES), BF16),
            pltpu.VMEM((1, CHIP_ROWS), F32),
            pltpu.VMEM((u, LANES), F32),
            seed_slots,
            pltpu.VMEM((Z * u, LANES), BF16),
            seed_slots,
            seed_slots,
            slots,
            pltpu.VMEM((2, Z * OWN, D + LANES), jnp.int16),
            slots,
            slots,
            pltpu.VMEM((2, 2 * HALF, D), BF16),
            pltpu.SemaphoreType.DMA((LOADS,)),
            pltpu.SemaphoreType.DMA((3, 18)),
            pltpu.SemaphoreType.DMA((3, 18)),
            pltpu.SemaphoreType.DMA((3, 32)),
            pltpu.SemaphoreType.DMA((3, 32)),
            pltpu.SemaphoreType.DMA((2, len(GROUPS), CENTS)),
            pltpu.SemaphoreType.DMA((2, len(GROUPS), CENTS)),
            pltpu.SemaphoreType.DMA((2, len(GROUPS))),
            pltpu.SemaphoreType.DMA((2, len(GROUPS))),
            pltpu.SemaphoreType.DMA((ROWS // PIECE,)),
            pltpu.SemaphoreType.DMA((ROWS // PIECE,)),
        ],
        compiler_params=pltpu.CompilerParams(
            collective_id=0, has_side_effects=True, vmem_limit_bytes=60 * 1024 * 1024
        ),
        cost_estimate=pl.CostEstimate(
            flops=8 * ROWS * CENT * D, bytes_accessed=POOL * D * 2, transcendentals=2 * ROWS * CENT
        ),
    )(embedding_pool, select_index, seed_index)
    return pl.pallas_call(
        hand_on,
        out_shape=(
            jax.ShapeDtypeStruct((CENT, D), BF16),
            jax.ShapeDtypeStruct((ROWS,), F32),
        ),
        in_specs=[vmem, vmem],
        out_specs=(vmem, vmem),
        cost_estimate=pl.CostEstimate(flops=0, bytes_accessed=4 * CENT * D + 8 * ROWS, transcendentals=0),
    )(centers, energy.reshape(ROWS))


def solution(mesh):
    placed = (P("row", None), P("row"), P("cent"))
    return jax.shard_map(
        on_device,
        mesh=mesh,
        in_specs=placed,
        out_specs=(P("cent", None), P("row")),
        check_vma=False,
    )
```

```python
import jax
import jax.numpy as jnp
from jax import lax
from jax.experimental import pallas as pl
from jax.experimental.pallas import tpu as pltpu
from jax.sharding import PartitionSpec as P

F32 = jnp.float32
BF16 = jnp.bfloat16
MESH = pl.DeviceIdType.MESH

POOL = 8192
ROWS = 4096
CENT = 512
CHIP_ROWS = 2 * ROWS
HALF = CENT // 4
D = 512
LANES = 128
PARTS = D // LANES
LOADS = 16
BLOCK = 1024
BLOCKS = CHIP_ROWS // BLOCK
PIECE = 1024
GROUPS = ((0, 2), (2, 4), (4, 7), (7, 8))
GROUP = 3 * BLOCK
JOINS = {4: (0,), 6: (1,), 7: (2, 3)}
OWN = 16
Z = 8
CENTS = 8
FAR_FIRST = (4, 3, 5, 2, 6, 1, 7)
NEAR_FIRST = FAR_FIRST[::-1]


def rows(start, size):
    return pl.ds(pl.multiple_of(start, size), size)


def log_sum(logs):
    top = logs[0]
    for other in logs[1:]:
        top = jnp.maximum(top, other)
    total = jnp.exp(logs[0] - top)
    for other in logs[1:]:
        total = total + jnp.exp(other - top)
    return top + jnp.log(total)


def normalize(v):
    return v * lax.rsqrt(jnp.sum(v * v, axis=1, keepdims=True) + 1e-06)


def pack(v):
    top = jnp.maximum(jnp.max(jnp.abs(v), axis=1, keepdims=True), 1e-30)
    exponent = jnp.ceil(jnp.log2(top))
    coded = jnp.round(v * (jnp.exp2(15.0 - exponent) * 0.999)).astype(jnp.int32)
    exponent = jnp.broadcast_to(exponent, (v.shape[0], LANES)).astype(jnp.int32)
    return jnp.concatenate([coded, exponent], axis=1).astype(jnp.int16)


def unpack(w):
    w = w.astype(jnp.int32).astype(F32)
    unit = jnp.exp2(w[:, D:] - 15.0) * (1.0 / 0.999)
    return jnp.concatenate([w[:, t * LANES : (t + 1) * LANES] * unit for t in range(PARTS)], axis=1)


def kernel(
    pool_hbm,
    select_hbm,
    seed_hbm,
    centers_out,
    energy_out,
    select,
    seed,
    pool_in,
    pool32,
    sample32,
    sample,
    seeds32,
    expo,
    scores,
    local,
    pair,
    stats,
    scale,
    sums,
    seeds16,
    core16,
    energy,
    own32,
    x_rx0,
    x_tx0,
    z_rx0,
    z_tx0,
    x_rx,
    x_tx,
    z_rx,
    z_tx,
    centers,
    load_sem,
    index_sem,
    rs_send,
    rs_recv,
    ag_send,
    ag_recv,
    stat_send,
    stat_recv,
    pair_send,
    pair_recv,
    sample_send,
    sample_recv,
):
    row = lax.axis_index("row")
    cent = lax.axis_index("cent")
    xh = row // 16
    z = (row // 2) % Z
    core = row % 2

    def row_id(xh_, z_, core_):
        return xh_ * 16 + z_ * 2 + core_

    sibling = (row_id(xh, z, 1 - core), cent)
    across = (row_id(1 - xh, z, core), cent)

    def z_id(distance):
        return (row_id(xh, (z + distance) % Z, core), cent)

    def cent_id(distance):
        return (row, (cent + distance) % CENTS)

    sent = []

    def send(src, dst, send_sem, recv_sem, device):
        copy = pltpu.make_async_remote_copy(
            src_ref=src, dst_ref=dst, send_sem=send_sem, recv_sem=recv_sem,
            device_id=device, device_id_type=MESH,
        )
        copy.start()
        sent.append(copy)

    def drain():
        for copy in sent:
            copy.wait_send()
        sent.clear()

    def arrived(dst, send_sem, recv_sem, device):
        pltpu.make_async_remote_copy(
            src_ref=dst, dst_ref=dst, send_sem=send_sem, recv_sem=recv_sem,
            device_id=device, device_id_type=MESH,
        ).wait_recv()

    step = POOL // LOADS

    def load(i):
        part = rows(i * step, step)
        return pltpu.make_async_copy(pool_hbm.at[part], pool_in.at[part], load_sem.at[i])

    for i in range(LOADS // 4):
        load(i).start()
    indices = [
        pltpu.make_async_copy(select_hbm, select, index_sem.at[0]),
        pltpu.make_async_copy(seed_hbm, seed, index_sem.at[1]),
    ]
    for copy in indices:
        copy.start()
    barrier = pltpu.get_barrier_semaphore()
    partners = [z_id(d) for d in FAR_FIRST] + [cent_id(d) for d in range(1, CENTS)] + [across, sibling]
    for partner in partners:
        pl.semaphore_signal(barrier, inc=1, device_id=partner, device_id_type=MESH)
    for i in range(LOADS // 4, LOADS):
        load(i).start()

    def widen(i, carry):
        load(i).wait()
        for b in range(step // 128):
            start = pl.multiple_of(i * step + b * 128, 128)
            block = pool_in[pl.ds(start, 128), :].astype(F32)
            for t in range(PARTS):
                pool32[pl.ds(start * PARTS + t, 128, stride=PARTS), :] = block[:, t * LANES : (t + 1) * LANES]
        return carry

    lax.fori_loop(0, LOADS, widen, 0)
    for copy in indices:
        copy.wait()
    pool32[POOL * PARTS :, :] = jnp.zeros((2 * PARTS, LANES), F32)

    def pick_seed(b, carry):
        for v in range(16):
            k = b * 16 + v
            where = seed[k]
            away = lax.shift_right_arithmetic(where, 12) - row
            away = jnp.minimum(jnp.maximum(away, -away), 1)
            index = select[jnp.bitwise_and(where, ROWS - 1)]
            index = index + (POOL - index) * away
            seeds32[pl.ds(pl.multiple_of(k * PARTS, PARTS), PARTS), :] = pool32[pl.ds(index * PARTS, PARTS), :]
        return carry

    lax.fori_loop(0, CENT // 16, pick_seed, 0)
    seeds16[...] = seeds32[...].astype(BF16)

    def gather_piece(p):
        def gather(b, carry):
            for v in range(64):
                i = b * 64 + v
                index = select[p * PIECE + i]
                sample32[pl.ds(pl.multiple_of(i * PARTS, PARTS), PARTS), :] = pool32[
                    pl.ds(index * PARTS, PARTS), :
                ]
            return carry

        def narrow(b, carry):
            start = b * 128
            for t in range(PARTS):
                sample[rows(core * ROWS + p * PIECE + start, 128), t * LANES : (t + 1) * LANES] = sample32[
                    pl.ds(start * PARTS + t, 128, stride=PARTS), :
                ].astype(BF16)
            return carry

        lax.fori_loop(0, PIECE // 64, gather, 0)
        lax.fori_loop(0, PIECE // 128, narrow, 0)

    def gather_pieces(first, last):
        for p in range(first, last):
            gather_piece(p)

    def share_samples():
        for p in range(ROWS // PIECE):
            piece = sample.at[rows(core * ROWS + p * PIECE, PIECE)]
            send(piece, piece, sample_send.at[p], sample_recv.at[p], sibling)

    def beside_z():
        gather_pieces(2, 4)
        share_samples()

    def core_sems(phase, other):
        return rs_send.at[phase, 16 + other], rs_recv.at[phase, 16 + other]

    def reduce_scatter(phase, own, other, x_rx, x_tx, z_rx, z_tx, code, decode, beside_x=None, beside_z=None):
        def sems(i):
            return rs_send.at[phase, i], rs_recv.at[phase, i]

        u = x_rx.shape[1]
        x_tx[...] = code(other)
        for d in FAR_FIRST + (0,):
            send(x_tx.at[rows((z + d) % Z * u, u)], x_rx.at[d], *sems(d), across)
        if beside_x:
            beside_x()
        for d in FAR_FIRST + (0,):
            arrived(x_rx.at[d], *sems(d), across)
            total = own((z + d) % Z) + decode(x_rx[d])
            if d:
                z_tx[d] = code(total)
                send(z_tx.at[d], z_rx.at[d], *sems(8 + d), z_id(d))
        if beside_z:
            beside_z()
        for d in NEAR_FIRST:
            arrived(z_rx.at[d], *sems(8 + d), z_id(Z - d))
            total = total + decode(z_rx[d])
        return total

    def part(dst, xh_, z_, core_):
        return dst.at[rows(xh_ * (2 * HALF) + core_ * HALF + z_ * OWN, OWN)]

    def ag_sems(phase, i):
        return ag_send.at[phase, i], ag_recv.at[phase, i]

    def scored(dst, side, d):
        return dst.at[rows(side * HALF + (z - d + Z) % Z * OWN, OWN)]

    def spread_near(phase, dst):
        mine = scored(dst, 0, 0)
        for d in FAR_FIRST:
            send(mine, mine, *ag_sems(phase, d), z_id(d))
        send(mine, scored(dst, 1, 0), *ag_sems(phase, 8), across)
        for d in NEAR_FIRST:
            block = scored(dst, 0, d)
            arrived(block, *ag_sems(phase, d), z_id(Z - d))
            send(block, scored(dst, 1, d), *ag_sems(phase, 8 + d), across)

    def spread_far(phase, dst):
        for d in (0,) + NEAR_FIRST:
            arrived(scored(dst, 1, d), *ag_sems(phase, 8 + d), across)

    def gather_near(phase, dst, beside=None):
        mine = part(dst, xh, z, core)
        for d in FAR_FIRST:
            send(mine, mine, *ag_sems(phase, d), z_id(d))
        send(mine, mine, *ag_sems(phase, 8), across)
        send(mine, mine, *ag_sems(phase, 16), sibling)
        if beside:
            beside()
        for d in NEAR_FIRST:
            block = part(dst, xh, (z - d + Z) % Z, core)
            arrived(block, *ag_sems(phase, d), z_id(Z - d))
            send(block, block, *ag_sems(phase, 8 + d), across)
            send(block, block, *ag_sems(phase, 16 + d), sibling)
        for d in (0,) + NEAR_FIRST:
            arrived(part(dst, xh, (z - d + Z) % Z, 1 - core), *ag_sems(phase, 16 + d), sibling)

    def pass_on(phase, dst, i):
        d = ((0,) + NEAR_FIRST)[i]
        block = part(dst, 1 - xh, (z - d + Z) % Z, core)
        arrived(block, *ag_sems(phase, 8 + d), across)
        send(block, block, *ag_sems(phase, 24 + d), sibling)

    def gather_far(phase, dst):
        for d in (0,) + NEAR_FIRST:
            arrived(part(dst, 1 - xh, (z - d + Z) % Z, 1 - core), *ag_sems(phase, 24 + d), sibling)

    u = OWN * PARTS
    pl.semaphore_wait(barrier, len(partners))
    for other in (1, 0):
        side = (1 - xh) if other else xh
        send(
            seeds16.at[rows((side * 2 + 1 - core) * Z * u, Z * u)], core16.at[other],
            *core_sems(0, other), sibling,
        )

    arrived(core16.at[1], *core_sems(0, 1), sibling)

    def beside_x():
        gather_pieces(0, 2)
        arrived(core16.at[0], *core_sems(0, 0), sibling)

    def own_seeds(w):
        return (seeds16[rows((xh * 2 + core) * Z * u + w * u, u), :].astype(F32)
                + core16[0, rows(w * u, u), :].astype(F32))

    other_seeds = seeds16[rows(((1 - xh) * 2 + core) * Z * u, Z * u), :].astype(F32) + core16[1].astype(F32)

    own32[...] = reduce_scatter(
        0, own_seeds, other_seeds, x_rx0, x_tx0, z_rx0, z_tx0,
        lambda v: v.astype(BF16), lambda v: v.astype(F32),
        beside_x, beside_z,
    )
    seeded = jnp.concatenate([own32[pl.ds(t, OWN, stride=PARTS), :] for t in range(PARTS)], axis=1)
    centers[0, rows(z * OWN, OWN), :] = normalize(seeded).astype(BF16)
    spread_near(0, centers.at[0])
    for p in range(ROWS // PIECE):
        arrived(
            sample.at[rows((1 - core) * ROWS + p * PIECE, PIECE)], sample_send.at[p], sample_recv.at[p], sibling
        )

    for it in range(2):
        current = centers.at[it]

        def stats_of(g, d):
            first, last = GROUPS[g]
            return stats.at[it, g, d, :, pl.ds(0, (last - first) * BLOCK)]

        def score(side, j):
            scores[j % 2] = lax.dot_general(
                current[side * HALF : (side + 1) * HALF, :], sample[j * BLOCK : (j + 1) * BLOCK, :],
                (((1,), (1,)), ((), ())), preferred_element_type=F32,
            )

        def soften(side, j):
            slot = j % 2
            top = [scores[slot, 8 * i : 8 * i + 8, :] for i in range(2)]
            for i in range(2, HALF // 8):
                top[i % 2] = jnp.maximum(top[i % 2], scores[slot, 8 * i : 8 * i + 8, :])
            top = jnp.max(jnp.maximum(top[0], top[1]), axis=0, keepdims=True)
            total = [jnp.zeros((8, BLOCK), F32)] * 2
            for i in range(HALF // 8):
                e = jnp.exp(scores[slot, 8 * i : 8 * i + 8, :] - top)
                expo[j, side * HALF + 8 * i : side * HALF + 8 * i + 8, :] = e
                total[i % 2] = total[i % 2] + e
            total = jnp.sum(total[0] + total[1], axis=0, keepdims=True)
            columns = slice(j * BLOCK, (j + 1) * BLOCK)
            local[side, 0:1, columns] = top
            if side == 0:
                local[0, 1:2, columns] = total
            else:
                near = local[0, 0:1, columns]
                both = jnp.maximum(near, top)
                total = total * jnp.exp(top - both) + local[0, 1:2, columns] * jnp.exp(near - both)
                g = [first <= j < last for first, last in GROUPS].index(True)
                inside = slice((j - GROUPS[g][0]) * BLOCK, (j - GROUPS[g][0] + 1) * BLOCK)
                pair[it, g, 0, 0:1, inside] = both + jnp.log(total)

        def pair_of(g, c):
            first, last = GROUPS[g]
            return pair.at[it, g, c, :, pl.ds(0, (last - first) * BLOCK)]

        def join(g):
            arrived(pair_of(g, 1), pair_send.at[it, g], pair_recv.at[it, g], sibling)
            inside = slice(0, (GROUPS[g][1] - GROUPS[g][0]) * BLOCK)
            stats[it, g, 0, 0:1, inside] = log_sum([pair[it, g, c, 0:1, inside] for c in range(2)])
            for d in range(1, CENTS):
                send(stats_of(g, 0), stats_of(g, d), stat_send.at[it, g, d], stat_recv.at[it, g, d], cent_id(d))

        for side in (0, 1):
            if side:
                spread_far(it, current)
            score(side, 0)
            for j in range(BLOCKS):
                if j + 1 < BLOCKS:
                    score(side, j + 1)
                soften(side, j)
                if side and j + 1 in [last for _, last in GROUPS]:
                    g = [last for _, last in GROUPS].index(j + 1)
                    send(pair_of(g, 0), pair_of(g, 1), pair_send.at[it, g], pair_recv.at[it, g], sibling)
                if side:
                    for g in JOINS.get(j, ()):
                        join(g)

        def merge(g):
            for d in range(1, CENTS):
                arrived(
                    stats_of(g, d), stat_send.at[it, g, d], stat_recv.at[it, g, d], cent_id(CENTS - d)
                )
            first, last = GROUPS[g]
            size = (last - first) * BLOCK
            total = log_sum([stats[it, g, d, 0:1, 0:size] for d in range(CENTS)])
            columns = slice(first * BLOCK, last * BLOCK)
            for side in range(2):
                scale[side, 0:1, columns] = jnp.exp(local[side, 0:1, columns] - total)
            if it == 1:
                energy[0:1, columns] = total

        def add_up(g, sides):
            part = pl.ds(sides[0] * HALF, len(sides) * HALF)
            probs = jnp.concatenate(
                [
                    jnp.concatenate(
                        [
                            (expo[j, side * HALF : (side + 1) * HALF, :]
                             * scale[side, 0:1, j * BLOCK : (j + 1) * BLOCK]).astype(BF16)
                            for side in sides
                        ],
                        axis=0,
                    )
                    for j in range(*GROUPS[g])
                ],
                axis=1,
            )
            term = jnp.dot(
                probs, sample[GROUPS[g][0] * BLOCK : GROUPS[g][1] * BLOCK, :], preferred_element_type=F32
            )
            if g:
                sums[it, part, :] += term
            else:
                sums[it, part, :] = term

        def own_sums(w):
            return sums[it, rows(w * OWN, OWN), :]

        final = len(GROUPS) - 1
        for g in range(final):
            merge(g)
            add_up(g, (0, 1))
        merge(final)
        add_up(final, (1,))
        total = reduce_scatter(
            1 + it, own_sums, sums[it, HALF:, :],
            x_rx.at[it], x_tx.at[it], z_rx.at[it], z_tx.at[it], pack, unpack, lambda: add_up(final, (0,)), drain,
        )
        if it == 0:
            centers[1, rows(z * OWN, OWN), :] = normalize(total).astype(BF16)
            spread_near(1, centers.at[1])
    mine = rows(xh * (2 * HALF) + core * HALF + z * OWN, OWN)
    centers_out[mine, :] = normalize(total).astype(BF16)
    energy_out[...] = energy[:, rows(core * ROWS, ROWS)]
    gather_near(2, centers_out)
    for i in range(Z):
        pass_on(2, centers_out, i)
    drain()
    gather_far(2, centers_out)


def hand_on(centers_in, energy_in, centers_out, energy_out):
    centers_out[...] = centers_in[...]
    energy_out[...] = energy_in[...]


def on_device(embedding_pool, select_index, seed_index):
    vmem = pl.BlockSpec(memory_space=pltpu.VMEM)
    u = OWN * PARTS
    seed_slots = pltpu.VMEM((Z, u, LANES), BF16)
    slots = pltpu.VMEM((2, Z, OWN, D + LANES), jnp.int16)
    centers, energy = pl.pallas_call(
        kernel,
        out_shape=(
            jax.ShapeDtypeStruct((CENT, D), BF16),
            jax.ShapeDtypeStruct((1, ROWS), F32),
        ),
        in_specs=[pl.BlockSpec(memory_space=pl.ANY)] * 3,
        out_specs=(vmem, vmem),
        scratch_shapes=[
            pltpu.SMEM((ROWS,), jnp.int32),
            pltpu.SMEM((CENT,), jnp.int32),
            pltpu.VMEM((POOL, D), BF16),
            pltpu.VMEM(((POOL + 2) * PARTS, LANES), F32),
            pltpu.VMEM((PIECE * PARTS, LANES), F32),
            pltpu.VMEM((CHIP_ROWS, D), BF16),
            pltpu.VMEM((CENT * PARTS, LANES), F32),
            pltpu.VMEM((BLOCKS, 2 * HALF, BLOCK), F32),
            pltpu.VMEM((2, HALF, BLOCK), F32),
            pltpu.VMEM((2, 2, CHIP_ROWS), F32),
            pltpu.VMEM((2, len(GROUPS), 2, 1, GROUP), F32),
            pltpu.VMEM((2, len(GROUPS), CENTS, 1, GROUP), F32),
            pltpu.VMEM((2, 1, CHIP_ROWS), F32),
            pltpu.VMEM((2, 2 * HALF, D), F32),
            pltpu.VMEM((CENT * PARTS, LANES), BF16),
            pltpu.VMEM((2, Z * u, LANES), BF16),
            pltpu.VMEM((1, CHIP_ROWS), F32),
            pltpu.VMEM((u, LANES), F32),
            seed_slots,
            pltpu.VMEM((Z * u, LANES), BF16),
            seed_slots,
            seed_slots,
            slots,
            pltpu.VMEM((2, Z * OWN, D + LANES), jnp.int16),
            slots,
            slots,
            pltpu.VMEM((2, 2 * HALF, D), BF16),
            pltpu.SemaphoreType.DMA((LOADS,)),
            pltpu.SemaphoreType.DMA((2,)),
            pltpu.SemaphoreType.DMA((3, 18)),
            pltpu.SemaphoreType.DMA((3, 18)),
            pltpu.SemaphoreType.DMA((3, 32)),
            pltpu.SemaphoreType.DMA((3, 32)),
            pltpu.SemaphoreType.DMA((2, len(GROUPS), CENTS)),
            pltpu.SemaphoreType.DMA((2, len(GROUPS), CENTS)),
            pltpu.SemaphoreType.DMA((2, len(GROUPS))),
            pltpu.SemaphoreType.DMA((2, len(GROUPS))),
            pltpu.SemaphoreType.DMA((ROWS // PIECE,)),
            pltpu.SemaphoreType.DMA((ROWS // PIECE,)),
        ],
        compiler_params=pltpu.CompilerParams(
            collective_id=0, has_side_effects=True, vmem_limit_bytes=60 * 1024 * 1024
        ),
        cost_estimate=pl.CostEstimate(
            flops=8 * ROWS * CENT * D, bytes_accessed=POOL * D * 2, transcendentals=2 * ROWS * CENT
        ),
    )(embedding_pool, select_index, seed_index)
    return pl.pallas_call(
        hand_on,
        out_shape=(
            jax.ShapeDtypeStruct((CENT, D), BF16),
            jax.ShapeDtypeStruct((ROWS,), F32),
        ),
        in_specs=[vmem, vmem],
        out_specs=(vmem, vmem),
        cost_estimate=pl.CostEstimate(flops=0, bytes_accessed=4 * CENT * D + 8 * ROWS, transcendentals=0),
    )(centers, energy.reshape(ROWS))


def solution(mesh):
    placed = (P("row", None), P("row"), P("cent"))
    return jax.shard_map(
        on_device,
        mesh=mesh,
        in_specs=placed,
        out_specs=(P("cent", None), P("row")),
        check_vma=False,
    )
```
